32 devices in a mesh: seq: 16 (over z, y, core), head: 2 (over x).
Axes of the slice: x: 2, y: 2, z: 4, core: 2. Of those that a mesh axis runs over, the one named last changes fastest.
Arguments:
- tokens: bfloat16 [65536, 1024], P(('seq', 'head')), may hold values from -32 to 32
- w_qkv: bfloat16 [1024, 3072], P('seq'), may hold values from -0.1875 to 0.1875
- w_out: bfloat16 [1024, 1024], P('seq'), may hold values from -0.1875 to 0.1875
- neighbours: int32 [512, 12], P('seq'), may hold values from 0 to 511, as said below
Outputs:
- update: bfloat16 [65536, 1024], P(('seq', 'head'))
The draws below stay inside these ranges and needn't reach their ends.
Inputs may be any that keep to these rules, and one draw needn't show every extreme that they name: Block b has grid coordinates z = b // 16, y = (b // 4) % 4, x = b % 4. Each row lists b itself first, then 11 different blocks among its 26 neighbours at offsets -1, 0, 1 in each coordinate (z taken modulo 512 // 16, y and x modulo 4).
All inputs are finite; a program needn't handle non-finite values.
Results may differ from the reference program's by a relative error of at most 0.0065.
The reference program's roundings to bfloat16 on the way (of `qkv`, `probs` and `attended`) count: a program that leaves them out, or rounds other values in their place, can miss the bound.
Values may be sent and summed in bfloat16 or wider, within the bound.
No kernel may reach another device: no remote copies, remote signals or barrier semaphores. Data moves between devices by JAX's collectives and lax.ppermute only.
A program may use at most 128 MiB of HBM per device.

```python
import math
import jax
import jax.numpy as jnp
import numpy as np
from jax import lax

D = 1024
HEADS = 8
HD = 128
BLK = 128
NBR = 12
PB = 16
NBLK = 512
TOKENS = 65536


def offset_table():
    rows = []
    for step_z in (-1, 0, 1):
        for step_y in (-1, 0, 1):
            for step_x in (-1, 0, 1):
                if step_z != 0 or step_y != 0 or step_x != 0:
                    rows.append([step_z, step_y, step_x])
    return np.array(rows, dtype=np.int32)


def draw_neighbours(key, part):
    depth = NBLK // PB
    blocks = jnp.arange(NBLK, dtype=jnp.int32)
    coord_z = blocks // PB
    coord_y = blocks // 4 % 4
    coord_x = blocks % 4
    table = jnp.asarray(offset_table())
    scores = jax.random.randint(key, (NBLK, 26), 0, 1 << 20) * 32 + jnp.arange(26, dtype=jnp.int32)
    unused, picks = lax.top_k(scores, NBR - 1)
    chosen = table[picks]
    near_z = jnp.mod(coord_z[:, None] + chosen[:, :, 0], depth)
    near_y = jnp.mod(coord_y[:, None] + chosen[:, :, 1], 4)
    near_x = jnp.mod(coord_x[:, None] + chosen[:, :, 2], 4)
    others = near_z * PB + near_y * 4 + near_x
    return jnp.concatenate([blocks[:, None], others], axis=1).astype(jnp.int32)


def draw_tokens(key, part):
    values = jax.random.normal(key, (TOKENS, D), jnp.float32)
    return jnp.clip(values, -4.0, 4.0).astype(jnp.bfloat16)


def block_scale(rng, dims, cuts, low, high):
    def one(position, blocks):
        heights = jax.random.uniform(jax.random.fold_in(jax.random.fold_in(rng, 6), position), (blocks,), jnp.float32, low / len(cuts), high / len(cuts))
        return jnp.repeat(jnp.exp(heights), dims[position] // blocks).reshape((-1,) + (1,) * (len(dims) - position - 1))

    loudness = one(*cuts[0])
    for cut in cuts[1:]:
        loudness = loudness * one(*cut)
    return loudness


def scatter_about(rng, extent, deviation, most, cuts=(), held_as=jnp.bfloat16):
    drawn = jax.random.normal(rng, extent, jnp.float32) * deviation
    if len(cuts) > 0:
        drawn = block_scale(rng, extent, cuts, -0.22, 0.18) * drawn
    return jnp.clip(drawn, min=-most, max=most).astype(held_as)


def setup_inputs(seed: int = 0) -> dict:
    seeds = jax.random.split(jax.random.key(seed), 5)
    tokens = draw_tokens(jax.random.fold_in(seeds[4], 71), 0)
    w_qkv = scatter_about(seeds[1], (D, 3 * D), D ** -0.5, 0.1875, ((0, 16),))
    w_out = scatter_about(seeds[2], (D, D), D ** -0.5, 0.1875, ((0, 16),))
    neighbours = draw_neighbours(jax.random.fold_in(seeds[4], 71), 0)
    return dict(tokens=tokens, w_qkv=w_qkv, w_out=w_out, neighbours=neighbours)


def reference(tokens, w_qkv, w_out, neighbours):
    planes = tokens.reshape(NBLK // PB, PB * BLK, D)

    def project(rows):
        return jnp.dot(rows, w_qkv, preferred_element_type=jnp.float32).astype(jnp.bfloat16)
    qkv = lax.map(project, planes).reshape(NBLK, BLK, 3, HEADS, HD)
    qkv = jnp.transpose(qkv, (3, 2, 0, 1, 4))
    scale = 1.0 / math.sqrt(HD)
    lists = neighbours.reshape(NBLK // PB, PB, NBR)

    def one_head(parts):
        queries = parts[0].reshape(NBLK // PB, PB, BLK, HD)
        key_blocks = parts[1]
        value_blocks = parts[2]

        def one_plane(args):
            query_group, list_group = args
            keys = key_blocks[list_group].reshape(PB, NBR * BLK, HD)
            values = value_blocks[list_group].reshape(PB, NBR * BLK, HD)
            scores = jnp.einsum('nqd,nkd->nqk', query_group.astype(jnp.float32), keys.astype(jnp.float32)) * scale
            largest = lax.optimization_barrier(jnp.max(scores, axis=-1, keepdims=True))
            expo = jnp.exp(scores - largest)
            probs = (expo / lax.optimization_barrier(jnp.sum(expo, axis=-1, keepdims=True))).astype(jnp.bfloat16)
            return jnp.einsum('nqk,nkd->nqd', probs.astype(jnp.float32), values.astype(jnp.float32)).astype(jnp.bfloat16)
        return lax.map(one_plane, (queries, lists))
    attended = lax.map(one_head, qkv)
    attended = attended.reshape(HEADS, TOKENS, HD).transpose(1, 0, 2).reshape(TOKENS, D)
    return jnp.dot(attended, w_out, preferred_element_type=jnp.float32).astype(jnp.bfloat16)
```

```python
import functools
import math

import jax
import jax.numpy as jnp
from jax import lax
from jax.experimental import pallas as pl
from jax.experimental.pallas import tpu as pltpu
from jax.sharding import PartitionSpec as P

HEADS = 8
HD = 128
BLK = 128
NBR = 12
PB = 16
D = HEADS * HD
PLANE = PB * BLK
TILE = 512
CUTS = (192, 1216, 512, 128)
LARGE = 2.0**100
MIB = 1 << 20
VMEM_LIMIT = 54 * MIB


def project_kernel(x_ref, w_ref, q_ref, k_ref, vt_ref):
    x = x_ref[...]

    def part(start):
        product = jnp.dot(x, w_ref[:, start : start + 512], preferred_element_type=jnp.float32)
        return product.astype(jnp.bfloat16)

    for col in range(0, D, 512):
        q_ref[:, col : col + 512] = part(col)
        k_ref[:, col : col + 512] = part(D + col)
        vt_ref[col : col + 512, :] = part(2 * D + col).T


def project_cost(rows, columns):
    return pl.CostEstimate(
        flops=2 * rows * D * columns, bytes_accessed=2 * rows * (D + columns), transcendentals=0
    )


def project_own(x, w):
    rows = x.shape[0]
    row_spec = pl.BlockSpec((TILE, D), lambda i: (i, 0))
    return pl.pallas_call(
        project_kernel,
        grid=(rows // TILE,),
        in_specs=[row_spec, pl.BlockSpec(memory_space=pltpu.VMEM)],
        out_specs=[row_spec, row_spec, pl.BlockSpec((D, TILE), lambda i: (0, i))],
        out_shape=[
            jax.ShapeDtypeStruct((rows, D), jnp.bfloat16),
            jax.ShapeDtypeStruct((3 * PLANE, D), jnp.bfloat16),
            jax.ShapeDtypeStruct((D, 3 * PLANE), jnp.bfloat16),
        ],
        compiler_params=pltpu.CompilerParams(vmem_limit_bytes=VMEM_LIMIT),
        cost_estimate=project_cost(rows, 3 * D),
        name="project_qkv",
    )(x, w)


def project_halo_kernel(counts, bases, *refs):
    total = sum(counts)
    x_refs, (w_ref, _, _, k_hbm, vt_hbm, k_ref, vt_ref, k_sem, vt_sem) = refs[:total], refs[total:]
    copies = []
    at = 0
    offset = 0
    for i, count in enumerate(counts):
        pieces = [ref[...] for ref in x_refs[at : at + count]]
        at += count
        x = pieces[0] if count == 1 else jnp.concatenate(pieces, axis=0)
        size = x.shape[0]
        rows = pl.ds(offset, size)
        there = pl.ds(bases[i], size)
        offset += size
        for col in range(D, 2 * D, 512):
            part = jnp.dot(x, w_ref[:, col : col + 512], preferred_element_type=jnp.float32)
            k_ref[rows, col - D : col - D + 512] = part.astype(jnp.bfloat16)
        copies.append(pltpu.make_async_copy(k_ref.at[rows, :], k_hbm.at[there, :], k_sem.at[i]))
        copies[-1].start()
        for col in range(2 * D, 3 * D, 512):
            part = jnp.dot(x, w_ref[:, col : col + 512], preferred_element_type=jnp.float32)
            vt_ref[col - 2 * D : col - 2 * D + 512, rows] = part.astype(jnp.bfloat16).T
        copies.append(pltpu.make_async_copy(vt_ref.at[:, rows], vt_hbm.at[:, there], vt_sem.at[i]))
        copies[-1].start()
    for copy in copies:
        copy.wait()


def project_halo(groups, w, k, vt):
    counts = tuple(len(parts) for parts, _ in groups)
    bases = tuple(base for _, base in groups)
    xs = [part for parts, _ in groups for part in parts]
    rows = sum(x.shape[0] for x in xs)
    vmem = pl.BlockSpec(memory_space=pltpu.VMEM)
    hbm = pl.BlockSpec(memory_space=pltpu.HBM)
    return pl.pallas_call(
        functools.partial(project_halo_kernel, counts, bases),
        in_specs=[vmem] * (len(xs) + 1) + [hbm, hbm],
        out_specs=[hbm, hbm],
        out_shape=[
            jax.ShapeDtypeStruct(k.shape, jnp.bfloat16),
            jax.ShapeDtypeStruct(vt.shape, jnp.bfloat16),
        ],
        input_output_aliases={len(xs) + 1: 0, len(xs) + 2: 1},
        scratch_shapes=[
            pltpu.VMEM((rows, D), jnp.bfloat16),
            pltpu.VMEM((D, rows), jnp.bfloat16),
            pltpu.SemaphoreType.DMA((len(groups),)),
            pltpu.SemaphoreType.DMA((len(groups),)),
        ],
        compiler_params=pltpu.CompilerParams(vmem_limit_bytes=40 * MIB),
        cost_estimate=project_cost(rows, 2 * D),
        name="project_kv_halo",
    )(*xs, w, k, vt)


def update_kernel(early_tile, early_ref, rest_ref, w_ref, o_ref):
    def product(x_ref):
        x = x_ref[...]
        for col in range(0, D, 512):
            part = jnp.dot(x, w_ref[:, col : col + 512], preferred_element_type=jnp.float32)
            o_ref[:, col : col + 512] = part.astype(jnp.bfloat16)

    if early_tile is None:
        product(rest_ref)
        return

    @pl.when(pl.program_id(0) == early_tile)
    def _():
        product(early_ref)

    @pl.when(pl.program_id(0) != early_tile)
    def _():
        product(rest_ref)


def project_update(early, rest, w, early_tile):
    rows = rest.shape[0] + (0 if early_tile is None else early.shape[0])
    tiles = rows // TILE
    if early_tile is None:
        rest_map = lambda i: (i, 0)
    else:
        rest_map = lambda i: (jnp.minimum((i + tiles - early_tile - 1) % tiles, tiles - 2), 0)
    return pl.pallas_call(
        functools.partial(update_kernel, early_tile),
        grid=(tiles,),
        in_specs=[
            pl.BlockSpec((TILE, D), lambda i: (0, 0)),
            pl.BlockSpec((TILE, D), rest_map),
            pl.BlockSpec(memory_space=pltpu.VMEM),
        ],
        out_specs=pl.BlockSpec((TILE, D), lambda i: (i, 0)),
        out_shape=jax.ShapeDtypeStruct((rows, D), jnp.bfloat16),
        compiler_params=pltpu.CompilerParams(vmem_limit_bytes=VMEM_LIMIT),
        cost_estimate=project_cost(rows, D),
        name="project_update",
    )(early, rest, w)


def attend_kernel(first, blocks, lists_ref, q_ref, k_ref, vt_ref, o_ref, *scratch):
    s_ref, p_ref, m_ref, i_ref, l_ref = scratch
    factor = math.log2(math.e) / math.sqrt(HD)
    unroll = 4
    per = 4
    part_rows = per * BLK
    parts = NBR // per

    def listed(position):
        return lax.rem(first + position, q_ref.shape[0] // BLK)

    def starts_of(position):
        block = listed(position)
        return [pl.multiple_of(lists_ref[block, j] * BLK, BLK) for j in range(NBR)]

    def diagonal(position):
        q = q_ref[pl.ds(pl.multiple_of(listed(position) * BLK, BLK), BLK), :]
        zero = jnp.zeros((BLK, HD), jnp.bfloat16)
        return jnp.concatenate(
            [
                jnp.concatenate([q[:, :HD], zero], axis=1),
                jnp.concatenate([zero, q[:, HD:]], axis=1),
            ],
            axis=0,
        )

    def score_part(diag, starts, part):
        keys = jnp.concatenate(
            [k_ref[pl.ds(start, BLK), :] for start in starts[part * per : (part + 1) * per]], axis=0
        )
        return lax.dot_general(
            keys, diag, (((1,), (1,)), ((), ())), preferred_element_type=jnp.float32
        )

    def folded(x, reduce):
        return reduce(x.reshape(part_rows // 8, 8, 2 * BLK), axis=0)

    def expo_part(scores, slot, part, largest):
        expo = jnp.exp2((scores - largest) * factor)
        p_ref[slot, part * part_rows : (part + 1) * part_rows, :] = expo.astype(jnp.bfloat16)
        return folded(expo, jnp.sum)

    def value_product(position, slot, starts):
        values = jnp.concatenate([vt_ref[:, pl.ds(start, BLK)] for start in starts], axis=1)
        out = jnp.dot(values, p_ref[slot], preferred_element_type=jnp.float32)
        for h in range(2):
            part = slice(h * HD, (h + 1) * HD)
            mine = out[part, part] * i_ref[slot, :, part]
            rows = pl.ds(pl.multiple_of(position * BLK, BLK), BLK)
            o_ref[rows, part] = mine.T.astype(jnp.bfloat16)

    def first_part(position, slot):
        scores = score_part(diagonal(position), starts_of(position), 0)
        s_ref[slot] = scores
        m_ref[slot] = folded(scores, jnp.max)

    def step(position, slot):
        largest = jnp.max(m_ref[slot], axis=0, keepdims=True)
        previous = jnp.maximum(position - 1, 0)
        diag = diagonal(position)
        starts = starts_of(position)
        total = expo_part(s_ref[slot], slot, 0, largest)
        first_part(jnp.minimum(position + 1, blocks - 1), 1 - slot)
        for part in range(1, parts):
            total = total + expo_part(score_part(diag, starts, part), slot, part, largest)
            if part == 1:
                value_product(previous, 1 - slot, starts_of(previous))
        row_sum = jnp.sum(total, axis=0, keepdims=True)
        i_ref[slot] = 1.0 / row_sum
        l_ref[...] = jnp.maximum(l_ref[...], row_sum)

    @pl.when(pl.program_id(0) == 0)
    def _():
        p_ref[1] = jnp.zeros_like(p_ref[1])
        i_ref[1] = jnp.zeros_like(i_ref[1])

    l_ref[...] = jnp.zeros_like(l_ref)
    first_part(0, 0)

    @pl.loop(0, blocks // unroll)
    def _(index):
        for i in range(unroll):
            step(index * unroll + i, i % 2)

    value_product(blocks - 1, 1, starts_of(blocks - 1))

    @pl.when(jnp.logical_not(jnp.max(l_ref[...]) < LARGE))
    def _():
        @pl.loop(0, blocks)
        def _(position):
            diag = diagonal(position)
            starts = starts_of(position)
            top = None
            for part in range(parts):
                scores = score_part(diag, starts, part)
                s_ref[part] = scores
                some = folded(scores, jnp.max)
                top = some if top is None else jnp.maximum(top, some)
            largest = jnp.max(top, axis=0, keepdims=True)
            total = None
            for part in range(parts):
                some = expo_part(s_ref[part], 1, part, largest)
                total = some if total is None else total + some
            i_ref[1] = 1.0 / jnp.sum(total, axis=0, keepdims=True)
            value_product(position, 1, starts)


def attend(lists, q, k, vt, first, blocks):
    rows = blocks * BLK
    pair = 2 * HD
    keys = NBR * BLK
    return pl.pallas_call(
        functools.partial(attend_kernel, first, blocks),
        grid_spec=pltpu.PrefetchScalarGridSpec(
            num_scalar_prefetch=1,
            grid=(D // pair,),
            in_specs=[
                pl.BlockSpec((q.shape[0], pair), lambda i, lists: (0, i)),
                pl.BlockSpec((3 * PLANE, pair), lambda i, lists: (0, i)),
                pl.BlockSpec((pair, 3 * PLANE), lambda i, lists: (i, 0)),
            ],
            out_specs=pl.BlockSpec((rows, pair), lambda i, lists: (0, i)),
            scratch_shapes=[
                pltpu.VMEM((3, keys // 3, pair), jnp.float32),
                pltpu.VMEM((2, keys, pair), jnp.bfloat16),
                pltpu.VMEM((2, 8, pair), jnp.float32),
                pltpu.VMEM((2, 1, pair), jnp.float32),
                pltpu.VMEM((1, pair), jnp.float32),
            ],
        ),
        out_shape=jax.ShapeDtypeStruct((rows, D), jnp.bfloat16),
        compiler_params=pltpu.CompilerParams(vmem_limit_bytes=VMEM_LIMIT),
        cost_estimate=pl.CostEstimate(
            flops=4 * rows * keys * D, bytes_accessed=32 * MIB, transcendentals=rows * keys * HEADS
        ),
        name="attend",
    )(lists, q, k, vt)


def local(tokens, w_qkv, w_out, neighbours):
    head_count = lax.axis_size("head")
    seq_count = lax.axis_size("seq")
    rows = tokens.shape[0]
    blocks = rows // BLK
    seq = lax.axis_index("seq")
    head = lax.axis_index("head")
    per_plane = PLANE // rows
    side = head // per_plane
    plane = 2 * seq + side
    tie = lax.optimization_barrier

    hops = []
    for s in range(seq_count):
        for h in range(head_count):
            step = 1 if h < per_plane else -1
            hops.append((s * head_count + h, (s + step) % seq_count * head_count + h))

    def forward(x):
        return lax.ppermute(x, ("seq", "head"), hops)

    planes = 2 * seq_count
    lists = lax.dynamic_slice_in_dim(neighbours, head * blocks, blocks, axis=0)
    offset = jnp.mod(lists // PB - plane + 1, planes) - 1
    toward = jnp.where(side == 0, 1, -1)
    slot = jnp.where(offset == 0, 0, jnp.where(offset == toward, 1, 2))
    lists = slot * PB + lists % PB

    w = lax.all_gather(w_qkv, "seq", axis=0, tiled=True)

    if head_count != 2:
        slab = lax.all_gather(tokens, "head", axis=0, tiled=True)
        own = lax.dynamic_slice_in_dim(slab, side * PLANE, PLANE, axis=0)
        other = lax.dynamic_slice_in_dim(slab, (1 - side) * PLANE, PLANE, axis=0)
        far = forward(other)
        q, k, vt = project_own(own, w)
        k, vt = project_halo([([other], PLANE)], w, k, vt)
        k, vt = project_halo([([far], 2 * PLANE)], w, k, vt)
        q = lax.dynamic_slice_in_dim(q, head % per_plane * rows, rows, axis=0)
    else:
        cuts = [0]
        for size in CUTS:
            cuts.append(cuts[-1] + size)

        def swap(x):
            return lax.ppermute(x, "head", [(0, 1), (1, 0)])

        first = tokens[: cuts[1]]
        rest, first = tie((tokens, first))
        x_0 = swap(first)
        later = [rest[start:stop] for start, stop in zip(cuts[1:], cuts[2:])]
        x_0, *later = tie((x_0, *later))
        x_1, x_2, x_3 = [swap(part) for part in later]
        far_0, far_1 = forward(x_0), forward(x_1)
        q, k, vt = project_own(tokens, w)
        x_2, k, vt = tie((x_2, k, vt))
        far_2 = forward(x_2)
        k, vt = project_halo([([x_0, x_1], PLANE)], w, k, vt)
        x_3, k, vt = tie((x_3, k, vt))
        far_3 = forward(x_3)
        k, vt = project_halo(
            [([far_0, far_1], 2 * PLANE), ([x_2, x_3], PLANE + cuts[2])], w, k, vt
        )
        k, vt = project_halo([([far_2, far_3], 2 * PLANE + cuts[2])], w, k, vt)
    k, w_last = tie((k, w_out))
    w_last = lax.all_gather(w_last, "seq", axis=0, tiled=True)
    attended = attend(lists, q, k, vt, 0, blocks)
    return project_update(attended, attended, w_last, None)


def solution(mesh):
    return jax.shard_map(
        local,
        mesh=mesh,
        in_specs=(P(("seq", "head"), None), P("seq", None), P("seq", None), P("seq", None)),
        out_specs=P(("seq", "head"), None),
        check_vma=False,
    )
```

```python
import functools
import math

import jax
import jax.numpy as jnp
from jax import lax
from jax.experimental import pallas as pl
from jax.experimental.pallas import tpu as pltpu
from jax.sharding import PartitionSpec as P

HEADS = 8
HD = 128
BLK = 128
NBR = 12
PB = 16
D = HEADS * HD
PLANE = PB * BLK
TILE = 512
CUTS = (192, 960, 640, 256)
LARGE = 2.0**100
MIB = 1 << 20
VMEM_LIMIT = 54 * MIB


def project_kv_kernel(x_ref, w_ref, k_ref, vt_ref):
    x = x_ref[...]
    for col in range(0, D, 512):
        part = jnp.dot(x, w_ref[:, col : col + 512], preferred_element_type=jnp.float32)
        k_ref[:, col : col + 512] = part.astype(jnp.bfloat16)
        part = jnp.dot(x, w_ref[:, D + col : D + col + 512], preferred_element_type=jnp.float32)
        vt_ref[col : col + 512, :] = part.astype(jnp.bfloat16).T


def project_q_kernel(x_ref, w_ref, q_ref):
    x = x_ref[...]
    for col in range(0, D, 512):
        part = jnp.dot(x, w_ref[:, col : col + 512], preferred_element_type=jnp.float32)
        q_ref[:, col : col + 512] = part.astype(jnp.bfloat16)


def project_cost(rows, columns):
    return pl.CostEstimate(
        flops=2 * rows * D * columns, bytes_accessed=2 * rows * (D + columns), transcendentals=0
    )


def project_rows(x, w, with_kv):
    rows = x.shape[0]
    row_spec = pl.BlockSpec((TILE, D), lambda i: (i, 0))
    if with_kv:
        out_specs = [row_spec, pl.BlockSpec((D, TILE), lambda i: (0, i))]
        out_shape = [
            jax.ShapeDtypeStruct((3 * PLANE, D), jnp.bfloat16),
            jax.ShapeDtypeStruct((D, 3 * PLANE), jnp.bfloat16),
        ]
    else:
        out_specs = row_spec
        out_shape = jax.ShapeDtypeStruct((rows, D), jnp.bfloat16)
    return pl.pallas_call(
        project_kv_kernel if with_kv else project_q_kernel,
        grid=(rows // TILE,),
        in_specs=[row_spec, pl.BlockSpec(memory_space=pltpu.VMEM)],
        out_specs=out_specs,
        out_shape=out_shape,
        compiler_params=pltpu.CompilerParams(vmem_limit_bytes=VMEM_LIMIT),
        cost_estimate=project_cost(rows, w.shape[1]),
        name="project_kv" if with_kv else "project_q",
    )(x, w)


def project_halo_kernel(counts, bases, *refs):
    total = sum(counts)
    x_refs, (w_ref, _, _, k_hbm, vt_hbm, k_ref, vt_ref, k_sem, vt_sem) = refs[:total], refs[total:]
    copies = []
    at = 0
    offset = 0
    for i, count in enumerate(counts):
        pieces = [ref[...] for ref in x_refs[at : at + count]]
        at += count
        x = pieces[0] if count == 1 else jnp.concatenate(pieces, axis=0)
        size = x.shape[0]
        rows = pl.ds(offset, size)
        there = pl.ds(bases[i], size)
        offset += size
        for col in range(0, D, 512):
            part = jnp.dot(x, w_ref[:, col : col + 512], preferred_element_type=jnp.float32)
            k_ref[rows, col : col + 512] = part.astype(jnp.bfloat16)
        copies.append(pltpu.make_async_copy(k_ref.at[rows, :], k_hbm.at[there, :], k_sem.at[i]))
        copies[-1].start()
        for col in range(0, D, 512):
            part = jnp.dot(x, w_ref[:, D + col : D + col + 512], preferred_element_type=jnp.float32)
            vt_ref[col : col + 512, rows] = part.astype(jnp.bfloat16).T
        copies.append(pltpu.make_async_copy(vt_ref.at[:, rows], vt_hbm.at[:, there], vt_sem.at[i]))
        copies[-1].start()
    for copy in copies:
        copy.wait()


def project_halo(groups, w, k, vt):
    counts = tuple(len(parts) for parts, _ in groups)
    bases = tuple(base for _, base in groups)
    xs = [part for parts, _ in groups for part in parts]
    rows = sum(x.shape[0] for x in xs)
    vmem = pl.BlockSpec(memory_space=pltpu.VMEM)
    hbm = pl.BlockSpec(memory_space=pltpu.HBM)
    return pl.pallas_call(
        functools.partial(project_halo_kernel, counts, bases),
        in_specs=[vmem] * (len(xs) + 1) + [hbm, hbm],
        out_specs=[hbm, hbm],
        out_shape=[
            jax.ShapeDtypeStruct(k.shape, jnp.bfloat16),
            jax.ShapeDtypeStruct(vt.shape, jnp.bfloat16),
        ],
        input_output_aliases={len(xs) + 1: 0, len(xs) + 2: 1},
        scratch_shapes=[
            pltpu.VMEM((rows, D), jnp.bfloat16),
            pltpu.VMEM((D, rows), jnp.bfloat16),
            pltpu.SemaphoreType.DMA((len(groups),)),
            pltpu.SemaphoreType.DMA((len(groups),)),
        ],
        compiler_params=pltpu.CompilerParams(vmem_limit_bytes=40 * MIB),
        cost_estimate=project_cost(rows, 2 * D),
        name="project_kv_halo",
    )(*xs, w, k, vt)


def update_kernel(early_tile, early_ref, rest_ref, w_ref, o_ref):
    def product(x_ref):
        x = x_ref[...]
        for col in range(0, D, 512):
            part = jnp.dot(x, w_ref[:, col : col + 512], preferred_element_type=jnp.float32)
            o_ref[:, col : col + 512] = part.astype(jnp.bfloat16)

    if early_tile is None:
        product(rest_ref)
        return

    @pl.when(pl.program_id(0) == early_tile)
    def _():
        product(early_ref)

    @pl.when(pl.program_id(0) != early_tile)
    def _():
        product(rest_ref)


def project_update(early, rest, w, early_tile):
    rows = rest.shape[0] + (0 if early_tile is None else early.shape[0])
    tiles = rows // TILE
    if early_tile is None:
        rest_map = lambda i: (i, 0)
    else:
        rest_map = lambda i: (jnp.minimum((i + tiles - early_tile - 1) % tiles, tiles - 2), 0)
    return pl.pallas_call(
        functools.partial(update_kernel, early_tile),
        grid=(tiles,),
        in_specs=[
            pl.BlockSpec((TILE, D), lambda i: (0, 0)),
            pl.BlockSpec((TILE, D), rest_map),
            pl.BlockSpec(memory_space=pltpu.VMEM),
        ],
        out_specs=pl.BlockSpec((TILE, D), lambda i: (i, 0)),
        out_shape=jax.ShapeDtypeStruct((rows, D), jnp.bfloat16),
        compiler_params=pltpu.CompilerParams(vmem_limit_bytes=VMEM_LIMIT),
        cost_estimate=project_cost(rows, D),
        name="project_update",
    )(early, rest, w)


def attend_kernel(first, blocks, lists_ref, q_ref, k_ref, vt_ref, o_ref, *scratch):
    s_ref, p_ref, m_ref, l_ref = scratch
    factor = math.log2(math.e) / math.sqrt(HD)
    unroll = 4
    edges = (0, 2, 7, 12)
    parts = len(edges) - 1

    def listed(position):
        return lax.rem(first + position, q_ref.shape[0] // BLK)

    def starts_of(position):
        block = listed(position)
        return [pl.multiple_of(lists_ref[block, j] * BLK, BLK) for j in range(NBR)]

    def diagonal(position):
        q = q_ref[pl.ds(pl.multiple_of(listed(position) * BLK, BLK), BLK), :]
        zero = jnp.zeros((BLK, HD), jnp.bfloat16)
        return jnp.concatenate(
            [
                jnp.concatenate([q[:, :HD], zero], axis=1),
                jnp.concatenate([zero, q[:, HD:]], axis=1),
            ],
            axis=0,
        )

    def score_part(diag, starts, part):
        keys = jnp.concatenate(
            [k_ref[pl.ds(start, BLK), :] for start in starts[edges[part] : edges[part + 1]]], axis=0
        )
        return lax.dot_general(
            keys, diag, (((1,), (1,)), ((), ())), preferred_element_type=jnp.float32
        )

    def folded_max(x):
        return jnp.max(x.reshape(x.shape[0] // 8, 8, 2 * BLK), axis=0)

    def expo_part(scores, slot, part, largest):
        expo = jnp.exp2((scores - largest) * factor)
        p_ref[slot, edges[part] * BLK : edges[part + 1] * BLK, :] = expo.astype(jnp.bfloat16)

    def value_product(position, slot):
        starts = starts_of(position)
        values = jnp.concatenate([vt_ref[:, pl.ds(start, BLK)] for start in starts], axis=1)
        values = jnp.concatenate([values, jnp.ones((16, NBR * BLK), jnp.bfloat16)], axis=0)
        out = jnp.dot(values, p_ref[slot], preferred_element_type=jnp.float32)
        row_sum = out[2 * HD : 2 * HD + 1, :]
        inverse = 1.0 / row_sum
        for h in range(2):
            part = slice(h * HD, (h + 1) * HD)
            mine = out[part, part] * inverse[:, part]
            rows = pl.ds(pl.multiple_of(position * BLK, BLK), BLK)
            o_ref[rows, part] = mine.T.astype(jnp.bfloat16)
        return row_sum

    def first_part(position, slot):
        scores = score_part(diagonal(position), starts_of(position), 0)
        s_ref[slot, : scores.shape[0], :] = scores
        m_ref[slot] = folded_max(scores)

    def step(position, slot):
        largest = jnp.max(m_ref[slot], axis=0, keepdims=True)
        diag = diagonal(position)
        starts = starts_of(position)
        expo_part(s_ref[slot, : edges[1] * BLK, :], slot, 0, largest)
        first_part(jnp.minimum(position + 1, blocks - 1), 1 - slot)
        for part in range(1, parts):
            expo_part(score_part(diag, starts, part), slot, part, largest)
            if part == 1:
                row_sum = value_product(jnp.maximum(position - 1, 0), 1 - slot)
                l_ref[...] = jnp.maximum(l_ref[...], row_sum)

    @pl.when(pl.program_id(0) == 0)
    def _():
        p_ref[1] = jnp.ones_like(p_ref[1])

    l_ref[...] = jnp.zeros_like(l_ref)
    first_part(0, 0)

    @pl.loop(0, blocks // unroll)
    def _(index):
        for i in range(unroll):
            step(index * unroll + i, i % 2)

    row_sum = value_product(blocks - 1, 1)
    row_sum = jnp.maximum(l_ref[...], row_sum)

    @pl.when(jnp.logical_not(jnp.max(row_sum) < LARGE))
    def _():
        @pl.loop(0, blocks)
        def _(position):
            diag = diagonal(position)
            starts = starts_of(position)
            top = None
            for part in range(parts):
                scores = score_part(diag, starts, part)
                s_ref[part, : scores.shape[0], :] = scores
                some = folded_max(scores)
                top = some if top is None else jnp.maximum(top, some)
            largest = jnp.max(top, axis=0, keepdims=True)
            for part in range(parts):
                size = (edges[part + 1] - edges[part]) * BLK
                expo_part(s_ref[part, :size, :], 1, part, largest)
            value_product(position, 1)


def attend(lists, q, k, vt, first, blocks):
    rows = blocks * BLK
    pair = 2 * HD
    keys = NBR * BLK
    return pl.pallas_call(
        functools.partial(attend_kernel, first, blocks),
        grid_spec=pltpu.PrefetchScalarGridSpec(
            num_scalar_prefetch=1,
            grid=(D // pair,),
            in_specs=[
                pl.BlockSpec((q.shape[0], pair), lambda i, lists: (0, i)),
                pl.BlockSpec((3 * PLANE, pair), lambda i, lists: (0, i)),
                pl.BlockSpec((pair, 3 * PLANE), lambda i, lists: (i, 0)),
            ],
            out_specs=pl.BlockSpec((rows, pair), lambda i, lists: (0, i)),
            scratch_shapes=[
                pltpu.VMEM((3, 5 * BLK, pair), jnp.float32),
                pltpu.VMEM((2, keys, pair), jnp.bfloat16),
                pltpu.VMEM((2, 8, pair), jnp.float32),
                pltpu.VMEM((1, pair), jnp.float32),
            ],
        ),
        out_shape=jax.ShapeDtypeStruct((rows, D), jnp.bfloat16),
        compiler_params=pltpu.CompilerParams(vmem_limit_bytes=VMEM_LIMIT),
        cost_estimate=pl.CostEstimate(
            flops=4 * rows * keys * D, bytes_accessed=32 * MIB, transcendentals=rows * keys * HEADS
        ),
        name="attend",
    )(lists, q, k, vt)


def local(tokens, w_qkv, w_out, neighbours):
    head_count = lax.axis_size("head")
    seq_count = lax.axis_size("seq")
    rows = tokens.shape[0]
    blocks = rows // BLK
    seq = lax.axis_index("seq")
    head = lax.axis_index("head")
    per_plane = PLANE // rows
    side = head // per_plane
    plane = 2 * seq + side
    tie = lax.optimization_barrier

    hops = []
    for s in range(seq_count):
        for h in range(head_count):
            step = 1 if h < per_plane else -1
            hops.append((s * head_count + h, (s + step) % seq_count * head_count + h))

    def forward(x):
        return lax.ppermute(x, ("seq", "head"), hops)

    planes = 2 * seq_count
    lists = lax.dynamic_slice_in_dim(neighbours, head * blocks, blocks, axis=0)
    offset = jnp.mod(lists // PB - plane + 1, planes) - 1
    toward = jnp.where(side == 0, 1, -1)
    slot = jnp.where(offset == 0, 0, jnp.where(offset == toward, 1, 2))
    lists = slot * PB + lists % PB

    w_kv = lax.all_gather(w_qkv[:, D:], "seq", axis=0, tiled=True)
    w_q = lax.all_gather(w_qkv[:, :D], "seq", axis=0, tiled=True)

    if head_count != 2:
        slab = lax.all_gather(tokens, "head", axis=0, tiled=True)
        own = lax.dynamic_slice_in_dim(slab, side * PLANE, PLANE, axis=0)
        other = lax.dynamic_slice_in_dim(slab, (1 - side) * PLANE, PLANE, axis=0)
        far = forward(other)
        k, vt = project_rows(own, w_kv, True)
        k, vt = project_halo([([other], PLANE)], w_kv, k, vt)
        k, vt = project_halo([([far], 2 * PLANE)], w_kv, k, vt)
        q = project_rows(tokens, w_q, False)
    else:
        cuts = [0]
        for size in CUTS:
            cuts.append(cuts[-1] + size)

        def swap(x):
            return lax.ppermute(x, "head", [(0, 1), (1, 0)])

        first = tokens[: cuts[1]]
        rest, first = tie((tokens, first))
        x_0 = swap(first)
        later = [rest[start:stop] for start, stop in zip(cuts[1:], cuts[2:])]
        x_0, *later = tie((x_0, *later))
        x_1, x_2, x_3 = [swap(part) for part in later]
        far_0, far_1 = forward(x_0), forward(x_1)
        k, vt = project_rows(tokens, w_kv, True)
        x_1, k, vt = tie((x_1, k, vt))
        k, vt = project_halo([([x_0, x_1], PLANE)], w_kv, k, vt)
        k, vt = project_halo([([far_0, far_1], 2 * PLANE)], w_kv, k, vt)
        x_2, k, vt = tie((x_2, k, vt))
        far_2 = forward(x_2)
        k, vt = project_halo([([x_2], PLANE + cuts[2])], w_kv, k, vt)
        x_3, k, vt = tie((x_3, k, vt))
        far_3 = forward(x_3)
        q = project_rows(tokens, w_q, False)
        k, vt, q = tie((k, vt, q))
        k, vt = project_halo(
            [([x_3], PLANE + cuts[3]), ([far_2, far_3], 2 * PLANE + cuts[2])], w_kv, k, vt
        )
    k, w_last = tie((k, w_out))
    w_last = lax.all_gather(w_last, "seq", axis=0, tiled=True)
    attended = attend(lists, q, k, vt, 0, blocks)
    return project_update(attended, attended, w_last, None)


def solution(mesh):
    return jax.shard_map(
        local,
        mesh=mesh,
        in_specs=(P(("seq", "head"), None), P("seq", None), P("seq", None), P("seq", None)),
        out_specs=P(("seq", "head"), None),
        check_vma=False,
    )
```

```python
import functools
import math

import jax
import jax.numpy as jnp
from jax import lax
from jax.experimental import pallas as pl
from jax.experimental.pallas import tpu as pltpu
from jax.sharding import PartitionSpec as P

HEADS = 8
HD = 128
BLK = 128
NBR = 12
PB = 16
D = HEADS * HD
PLANE = PB * BLK
TILE = 512
UPDATE_TILE = 256
CUTS = (192, 1088, 512, 256)
LARGE = 2.0**100
MIB = 1 << 20
VMEM_LIMIT = 54 * MIB


def project_own_kernel(x_ref, w_ref, q_ref, k_ref, vt_ref):
    x = x_ref[...]

    def part(start):
        product = jnp.dot(x, w_ref[:, start : start + 512], preferred_element_type=jnp.float32)
        return product.astype(jnp.bfloat16)

    for col in range(0, D, 512):
        q_ref[:, col : col + 512] = part(col)
        k_ref[:, col : col + 512] = part(D + col)
        vt_ref[col : col + 512, :] = part(2 * D + col).T


def project_cost(rows, columns):
    return pl.CostEstimate(
        flops=2 * rows * D * columns, bytes_accessed=2 * rows * (D + columns), transcendentals=0
    )


def project_own(x, w):
    row_spec = pl.BlockSpec((TILE, D), lambda i: (i, 0))
    return pl.pallas_call(
        project_own_kernel,
        grid=(PLANE // TILE,),
        in_specs=[row_spec, pl.BlockSpec(memory_space=pltpu.VMEM)],
        out_specs=[row_spec, row_spec, pl.BlockSpec((D, TILE), lambda i: (0, i))],
        out_shape=[
            jax.ShapeDtypeStruct((PLANE, D), jnp.bfloat16),
            jax.ShapeDtypeStruct((3 * PLANE, D), jnp.bfloat16),
            jax.ShapeDtypeStruct((D, 3 * PLANE), jnp.bfloat16),
        ],
        compiler_params=pltpu.CompilerParams(vmem_limit_bytes=VMEM_LIMIT),
        cost_estimate=project_cost(PLANE, 3 * D),
        name="project_qkv",
    )(x, w)


def project_halo_kernel(counts, bases, *refs):
    total = sum(counts)
    x_refs, (w_ref, _, _, k_hbm, vt_hbm, k_ref, vt_ref, k_sem, vt_sem) = refs[:total], refs[total:]
    copies = []
    at = 0
    offset = 0
    for i, count in enumerate(counts):
        pieces = [ref[...] for ref in x_refs[at : at + count]]
        at += count
        x = pieces[0] if count == 1 else jnp.concatenate(pieces, axis=0)
        size = x.shape[0]
        rows = pl.ds(offset, size)
        there = pl.ds(bases[i], size)
        offset += size
        for col in range(0, D, 512):
            part = jnp.dot(
                x, w_ref[:, D + col : D + col + 512], preferred_element_type=jnp.float32
            )
            k_ref[rows, col : col + 512] = part.astype(jnp.bfloat16)
        copies.append(pltpu.make_async_copy(k_ref.at[rows, :], k_hbm.at[there, :], k_sem.at[i]))
        copies[-1].start()
        for col in range(0, D, 512):
            part = jnp.dot(
                x, w_ref[:, 2 * D + col : 2 * D + col + 512], preferred_element_type=jnp.float32
            )
            vt_ref[col : col + 512, rows] = part.astype(jnp.bfloat16).T
        copies.append(pltpu.make_async_copy(vt_ref.at[:, rows], vt_hbm.at[:, there], vt_sem.at[i]))
        copies[-1].start()
    for copy in copies:
        copy.wait()


def project_halo(groups, w, k, vt):
    counts = tuple(len(parts) for parts, _ in groups)
    bases = tuple(base for _, base in groups)
    xs = [part for parts, _ in groups for part in parts]
    rows = sum(x.shape[0] for x in xs)
    vmem = pl.BlockSpec(memory_space=pltpu.VMEM)
    hbm = pl.BlockSpec(memory_space=pltpu.HBM)
    return pl.pallas_call(
        functools.partial(project_halo_kernel, counts, bases),
        in_specs=[vmem] * (len(xs) + 1) + [hbm, hbm],
        out_specs=[hbm, hbm],
        out_shape=[
            jax.ShapeDtypeStruct(k.shape, jnp.bfloat16),
            jax.ShapeDtypeStruct(vt.shape, jnp.bfloat16),
        ],
        input_output_aliases={len(xs) + 1: 0, len(xs) + 2: 1},
        scratch_shapes=[
            pltpu.VMEM((rows, D), jnp.bfloat16),
            pltpu.VMEM((D, rows), jnp.bfloat16),
            pltpu.SemaphoreType.DMA((len(groups),)),
            pltpu.SemaphoreType.DMA((len(groups),)),
        ],
        compiler_params=pltpu.CompilerParams(vmem_limit_bytes=40 * MIB),
        cost_estimate=project_cost(rows, 2 * D),
        name="project_kv_halo",
    )(*xs, w, k, vt)


def update_kernel(x_ref, w_ref, o_ref):
    part = jnp.dot(x_ref[...], w_ref[...], preferred_element_type=jnp.float32)
    o_ref[...] = part.astype(jnp.bfloat16)


def project_update(x, w):
    rows = x.shape[0]
    return pl.pallas_call(
        update_kernel,
        grid=(rows // UPDATE_TILE,),
        in_specs=[
            pl.BlockSpec((UPDATE_TILE, D), lambda i: (i, 0)),
            pl.BlockSpec((D, D), lambda i: (0, 0), pipeline_mode=pl.Buffered(1)),
        ],
        out_specs=pl.BlockSpec((UPDATE_TILE, D), lambda i: (i, 0)),
        out_shape=jax.ShapeDtypeStruct((rows, D), jnp.bfloat16),
        compiler_params=pltpu.CompilerParams(vmem_limit_bytes=VMEM_LIMIT),
        cost_estimate=project_cost(rows, D),
        name="project_update",
    )(x, w)


def attend_kernel(first, blocks, lists_ref, q_ref, k_ref, vt_ref, o_ref, *scratch):
    s_ref, p_ref, m_ref, l_ref = scratch
    factor = math.log2(math.e) / math.sqrt(HD)
    unroll = 4
    edges = (0, 2, 7, 12)
    parts = len(edges) - 1

    def listed(position):
        return lax.rem(first + position, q_ref.shape[0] // BLK)

    def starts_of(position):
        block = listed(position)
        return [pl.multiple_of(lists_ref[block, j] * BLK, BLK) for j in range(NBR)]

    def diagonal(position):
        q = q_ref[pl.ds(pl.multiple_of(listed(position) * BLK, BLK), BLK), :]
        zero = jnp.zeros((BLK, HD), jnp.bfloat16)
        return jnp.concatenate(
            [
                jnp.concatenate([q[:, :HD], zero], axis=1),
                jnp.concatenate([zero, q[:, HD:]], axis=1),
            ],
            axis=0,
        )

    def score_part(diag, starts, part):
        keys = jnp.concatenate(
            [k_ref[pl.ds(start, BLK), :] for start in starts[edges[part] : edges[part + 1]]], axis=0
        )
        return lax.dot_general(
            keys, diag, (((1,), (1,)), ((), ())), preferred_element_type=jnp.float32
        )

    def folded_max(x):
        return jnp.max(x.reshape(x.shape[0] // 8, 8, 2 * BLK), axis=0)

    def expo_part(scores, slot, part, largest):
        expo = jnp.exp2((scores - largest) * factor)
        p_ref[slot, edges[part] * BLK : edges[part + 1] * BLK, :] = expo.astype(jnp.bfloat16)

    def value_product(position, slot):
        starts = starts_of(position)
        values = jnp.concatenate([vt_ref[:, pl.ds(start, BLK)] for start in starts], axis=1)
        values = jnp.concatenate([values, jnp.ones((16, NBR * BLK), jnp.bfloat16)], axis=0)
        out = jnp.dot(values, p_ref[slot], preferred_element_type=jnp.float32)
        row_sum = out[2 * HD : 2 * HD + 1, :]
        inverse = 1.0 / row_sum
        for h in range(2):
            part = slice(h * HD, (h + 1) * HD)
            mine = out[part, part] * inverse[:, part]
            rows = pl.ds(pl.multiple_of(position * BLK, BLK), BLK)
            o_ref[rows, part] = mine.T.astype(jnp.bfloat16)
        return row_sum

    def first_part(position, slot):
        scores = score_part(diagonal(position), starts_of(position), 0)
        s_ref[slot, : scores.shape[0], :] = scores
        m_ref[slot] = folded_max(scores)

    def step(position, slot):
        largest = jnp.max(m_ref[slot], axis=0, keepdims=True)
        diag = diagonal(position)
        starts = starts_of(position)
        expo_part(s_ref[slot, : edges[1] * BLK, :], slot, 0, largest)
        first_part(jnp.minimum(position + 1, blocks - 1), 1 - slot)
        for part in range(1, parts):
            expo_part(score_part(diag, starts, part), slot, part, largest)
            if part == 1:
                row_sum = value_product(jnp.maximum(position - 1, 0), 1 - slot)
                l_ref[...] = jnp.maximum(l_ref[...], row_sum)

    @pl.when(pl.program_id(0) == 0)
    def _():
        p_ref[1] = jnp.ones_like(p_ref[1])

    l_ref[...] = jnp.zeros_like(l_ref)
    first_part(0, 0)

    @pl.loop(0, blocks // unroll)
    def _(index):
        for i in range(unroll):
            step(index * unroll + i, i % 2)

    row_sum = value_product(blocks - 1, 1)
    row_sum = jnp.maximum(l_ref[...], row_sum)

    @pl.when(jnp.logical_not(jnp.max(row_sum) < LARGE))
    def _():
        @pl.loop(0, blocks)
        def _(position):
            diag = diagonal(position)
            starts = starts_of(position)
            top = None
            for part in range(parts):
                scores = score_part(diag, starts, part)
                s_ref[part, : scores.shape[0], :] = scores
                some = folded_max(scores)
                top = some if top is None else jnp.maximum(top, some)
            largest = jnp.max(top, axis=0, keepdims=True)
            for part in range(parts):
                size = (edges[part + 1] - edges[part]) * BLK
                expo_part(s_ref[part, :size, :], 1, part, largest)
            value_product(position, 1)


def attend(lists, q, k, vt, first, blocks):
    rows = blocks * BLK
    pair = 2 * HD
    keys = NBR * BLK
    return pl.pallas_call(
        functools.partial(attend_kernel, first, blocks),
        grid_spec=pltpu.PrefetchScalarGridSpec(
            num_scalar_prefetch=1,
            grid=(D // pair,),
            in_specs=[
                pl.BlockSpec((q.shape[0], pair), lambda i, lists: (0, i)),
                pl.BlockSpec((3 * PLANE, pair), lambda i, lists: (0, i)),
                pl.BlockSpec((pair, 3 * PLANE), lambda i, lists: (i, 0)),
            ],
            out_specs=pl.BlockSpec((rows, pair), lambda i, lists: (0, i)),
            scratch_shapes=[
                pltpu.VMEM((3, 5 * BLK, pair), jnp.float32),
                pltpu.VMEM((2, keys, pair), jnp.bfloat16),
                pltpu.VMEM((2, 8, pair), jnp.float32),
                pltpu.VMEM((1, pair), jnp.float32),
            ],
        ),
        out_shape=jax.ShapeDtypeStruct((rows, D), jnp.bfloat16),
        compiler_params=pltpu.CompilerParams(vmem_limit_bytes=VMEM_LIMIT),
        cost_estimate=pl.CostEstimate(
            flops=4 * rows * keys * D, bytes_accessed=32 * MIB, transcendentals=rows * keys * HEADS
        ),
        name="attend",
    )(lists, q, k, vt)


def local(tokens, w_qkv, w_out, neighbours):
    head_count = lax.axis_size("head")
    seq_count = lax.axis_size("seq")
    rows = tokens.shape[0]
    blocks = rows // BLK
    seq = lax.axis_index("seq")
    head = lax.axis_index("head")
    per_plane = PLANE // rows
    side = head // per_plane
    plane = 2 * seq + side
    tie = lax.optimization_barrier

    hops = []
    for s in range(seq_count):
        for h in range(head_count):
            step = 1 if h < per_plane else -1
            hops.append((s * head_count + h, (s + step) % seq_count * head_count + h))

    def forward(x):
        return lax.ppermute(x, ("seq", "head"), hops)

    planes = 2 * seq_count
    lists = lax.dynamic_slice_in_dim(neighbours, head * blocks, blocks, axis=0)
    offset = jnp.mod(lists // PB - plane + 1, planes) - 1
    toward = jnp.where(side == 0, 1, -1)
    slot = jnp.where(offset == 0, 0, jnp.where(offset == toward, 1, 2))
    lists = slot * PB + lists % PB

    w = lax.all_gather(w_qkv, "seq", axis=0, tiled=True)

    if head_count != 2:
        slab = lax.all_gather(tokens, "head", axis=0, tiled=True)
        own = lax.dynamic_slice_in_dim(slab, side * PLANE, PLANE, axis=0)
        other = lax.dynamic_slice_in_dim(slab, (1 - side) * PLANE, PLANE, axis=0)
        far = forward(other)
        q, k, vt = project_own(own, w)
        k, vt = project_halo([([other], PLANE)], w, k, vt)
        k, vt = project_halo([([far], 2 * PLANE)], w, k, vt)
        q = lax.dynamic_slice_in_dim(q, head % per_plane * rows, rows, axis=0)
    else:
        cuts = [0]
        for size in CUTS:
            cuts.append(cuts[-1] + size)

        def swap(x):
            return lax.ppermute(x, "head", [(0, 1), (1, 0)])

        first = tokens[: cuts[1]]
        rest, first = tie((tokens, first))
        x_0 = swap(first)
        later = [rest[start:stop] for start, stop in zip(cuts[1:], cuts[2:])]
        x_0, *later = tie((x_0, *later))
        x_1, x_2, x_3 = [swap(part) for part in later]
        far_0, far_1 = forward(x_0), forward(x_1)
        q, k, vt = project_own(tokens, w)
        x_2, k, vt = tie((x_2, k, vt))
        far_2 = forward(x_2)
        k, vt = project_halo([([x_0, x_1], PLANE)], w, k, vt)
        x_3, k, vt = tie((x_3, k, vt))
        far_3 = forward(x_3)
        k, vt = project_halo([([far_0, far_1], 2 * PLANE)], w, k, vt)
        k, vt = project_halo([([x_2, x_3], PLANE + cuts[2])], w, k, vt)
        k, vt = project_halo([([far_2, far_3], 2 * PLANE + cuts[2])], w, k, vt)
    k, w_last = tie((k, w_out))
    w_last = lax.all_gather(w_last, "seq", axis=0, tiled=True)
    attended = attend(lists, q, k, vt, 0, blocks)
    return project_update(attended, w_last)


def solution(mesh):
    return jax.shard_map(
        local,
        mesh=mesh,
        in_specs=(P(("seq", "head"), None), P("seq", None), P("seq", None), P("seq", None)),
        out_specs=P(("seq", "head"), None),
        check_vma=False,
    )
```

```python
import functools
import math

import jax
import jax.numpy as jnp
from jax import lax
from jax.experimental import pallas as pl
from jax.experimental.pallas import tpu as pltpu
from jax.sharding import PartitionSpec as P

HEADS = 8
HD = 128
BLK = 128
NBR = 12
PB = 16
D = HEADS * HD
PLANE = PB * BLK
TILE = 512
CUTS = (1280, 640, 128)
STEP = 512
LARGE = 2.0**100
MIB = 1 << 20
VMEM_LIMIT = 54 * MIB


def project_own_kernel(x_ref, other_ref, w_hbm, q_hbm, k_hbm, vt_hbm, *scratch):
    w_ref, q_ref, k_ref, vt_ref, w_sem, q_sem, k_sem, vt_sem = scratch
    loads = []
    for i in range(3 * D // STEP):
        columns = pl.ds(i * STEP, STEP)
        loads.append(
            pltpu.make_async_copy(w_hbm.at[:, columns], w_ref.at[:, columns], w_sem.at[i])
        )
        loads[-1].start()
    pending = set(range(len(loads)))
    own = x_ref.shape[0]
    total = own + other_ref.shape[0]
    copies = []

    def send(source, target, sem):
        copies.append(pltpu.make_async_copy(source, target, sem))
        copies[-1].start()

    for i, start in enumerate(range(0, total, TILE)):
        stop = min(start + TILE, total)
        rows = slice(start, stop)
        x = x_ref[rows, :] if start < own else other_ref[start - own : stop - own, :]

        def part(index, x=x):
            if index in pending:
                pending.remove(index)
                loads[index].wait()
            weights = w_ref[:, index * STEP : (index + 1) * STEP]
            return jnp.dot(x, weights, preferred_element_type=jnp.float32).astype(jnp.bfloat16)

        third = D // STEP
        if start < own:
            for j in range(third):
                q_ref[rows, j * STEP : (j + 1) * STEP] = part(j)
            send(q_ref.at[rows, :], q_hbm.at[rows, :], q_sem.at[i])
        for j in range(third):
            k_ref[rows, j * STEP : (j + 1) * STEP] = part(third + j)
        send(k_ref.at[rows, :], k_hbm.at[rows, :], k_sem.at[i])
        for j in range(third):
            vt_ref[j * STEP : (j + 1) * STEP, rows] = part(2 * third + j).T
        send(vt_ref.at[:, rows], vt_hbm.at[:, rows], vt_sem.at[i])
    for copy in copies:
        copy.wait()


def project_cost(rows, columns):
    return pl.CostEstimate(
        flops=2 * rows * D * columns, bytes_accessed=2 * rows * (D + columns), transcendentals=0
    )


def project_own(x, other, w):
    own = x.shape[0]
    total = own + other.shape[0]
    tiles = -(-total // TILE)
    vmem = pl.BlockSpec(memory_space=pltpu.VMEM)
    hbm = pl.BlockSpec(memory_space=pltpu.HBM)
    return pl.pallas_call(
        project_own_kernel,
        in_specs=[vmem, vmem, hbm],
        out_specs=[hbm, hbm, hbm],
        out_shape=[
            jax.ShapeDtypeStruct((own, D), jnp.bfloat16),
            jax.ShapeDtypeStruct((3 * PLANE, D), jnp.bfloat16),
            jax.ShapeDtypeStruct((D, 3 * PLANE), jnp.bfloat16),
        ],
        scratch_shapes=[
            pltpu.VMEM((D, 3 * D), jnp.bfloat16),
            pltpu.VMEM((own, D), jnp.bfloat16),
            pltpu.VMEM((total, D), jnp.bfloat16),
            pltpu.VMEM((D, total), jnp.bfloat16),
            pltpu.SemaphoreType.DMA((3 * D // STEP,)),
            pltpu.SemaphoreType.DMA((tiles,)),
            pltpu.SemaphoreType.DMA((tiles,)),
            pltpu.SemaphoreType.DMA((tiles,)),
        ],
        compiler_params=pltpu.CompilerParams(vmem_limit_bytes=48 * MIB),
        cost_estimate=project_cost(total, 3 * D),
        name="project_qkv",
    )(x, other, w)


def project_halo_kernel(counts, bases, *refs):
    total = sum(counts)
    x_refs, (w_ref, _, _, k_hbm, vt_hbm, k_ref, vt_ref, k_sem, vt_sem) = refs[:total], refs[total:]
    copies = []
    at = 0
    offset = 0
    for i, count in enumerate(counts):
        pieces = [ref[...] for ref in x_refs[at : at + count]]
        at += count
        x = pieces[0] if count == 1 else jnp.concatenate(pieces, axis=0)
        size = x.shape[0]
        rows = pl.ds(offset, size)
        there = pl.ds(bases[i], size)
        offset += size
        for col in range(0, D, 512):
            part = jnp.dot(
                x, w_ref[:, D + col : D + col + 512], preferred_element_type=jnp.float32
            )
            k_ref[rows, col : col + 512] = part.astype(jnp.bfloat16)
        copies.append(pltpu.make_async_copy(k_ref.at[rows, :], k_hbm.at[there, :], k_sem.at[i]))
        copies[-1].start()
        for col in range(0, D, 512):
            part = jnp.dot(
                x, w_ref[:, 2 * D + col : 2 * D + col + 512], preferred_element_type=jnp.float32
            )
            vt_ref[col : col + 512, rows] = part.astype(jnp.bfloat16).T
        copies.append(pltpu.make_async_copy(vt_ref.at[:, rows], vt_hbm.at[:, there], vt_sem.at[i]))
        copies[-1].start()
    for copy in copies:
        copy.wait()


def project_halo(groups, w, k, vt):
    counts = tuple(len(parts) for parts, _ in groups)
    bases = tuple(base for _, base in groups)
    xs = [part for parts, _ in groups for part in parts]
    rows = sum(x.shape[0] for x in xs)
    vmem = pl.BlockSpec(memory_space=pltpu.VMEM)
    hbm = pl.BlockSpec(memory_space=pltpu.HBM)
    return pl.pallas_call(
        functools.partial(project_halo_kernel, counts, bases),
        in_specs=[vmem] * (len(xs) + 1) + [hbm, hbm],
        out_specs=[hbm, hbm],
        out_shape=[
            jax.ShapeDtypeStruct(k.shape, jnp.bfloat16),
            jax.ShapeDtypeStruct(vt.shape, jnp.bfloat16),
        ],
        input_output_aliases={len(xs) + 1: 0, len(xs) + 2: 1},
        scratch_shapes=[
            pltpu.VMEM((rows, D), jnp.bfloat16),
            pltpu.VMEM((D, rows), jnp.bfloat16),
            pltpu.SemaphoreType.DMA((len(groups),)),
            pltpu.SemaphoreType.DMA((len(groups),)),
        ],
        compiler_params=pltpu.CompilerParams(vmem_limit_bytes=40 * MIB),
        cost_estimate=project_cost(rows, 2 * D),
        name="project_kv_halo",
    )(*xs, w, k, vt)


def update_kernel(x_ref, w_ref, o_ref):
    x = x_ref[...]
    for col in range(0, D, STEP):
        part = jnp.dot(x, w_ref[:, col : col + STEP], preferred_element_type=jnp.float32)
        o_ref[:, col : col + STEP] = part.astype(jnp.bfloat16)


def project_update(x, w):
    rows = x.shape[0]
    row_spec = pl.BlockSpec((TILE, D), lambda i: (i, 0))
    return pl.pallas_call(
        update_kernel,
        grid=(rows // TILE,),
        in_specs=[row_spec, pl.BlockSpec(memory_space=pltpu.VMEM)],
        out_specs=row_spec,
        out_shape=jax.ShapeDtypeStruct((rows, D), jnp.bfloat16),
        compiler_params=pltpu.CompilerParams(vmem_limit_bytes=VMEM_LIMIT),
        cost_estimate=project_cost(rows, D),
        name="project_update",
    )(x, w)


def attend_kernel(first, blocks, lists_ref, q_ref, k_ref, vt_ref, o_ref, *scratch):
    s_ref, p_ref, m_ref, l_ref = scratch
    factor = math.log2(math.e) / math.sqrt(HD)
    unroll = 4
    edges = (0, 2, 7, 12)
    parts = len(edges) - 1

    def listed(position):
        return lax.rem(first + position, q_ref.shape[0] // BLK)

    def starts_of(position):
        block = listed(position)
        return [pl.multiple_of(lists_ref[block, j] * BLK, BLK) for j in range(NBR)]

    def diagonal(position):
        q = q_ref[pl.ds(pl.multiple_of(listed(position) * BLK, BLK), BLK), :]
        zero = jnp.zeros((BLK, HD), jnp.bfloat16)
        return jnp.concatenate(
            [
                jnp.concatenate([q[:, :HD], zero], axis=1),
                jnp.concatenate([zero, q[:, HD:]], axis=1),
            ],
            axis=0,
        )

    def score_part(diag, starts, part):
        keys = jnp.concatenate(
            [k_ref[pl.ds(start, BLK), :] for start in starts[edges[part] : edges[part + 1]]], axis=0
        )
        return lax.dot_general(
            keys, diag, (((1,), (1,)), ((), ())), preferred_element_type=jnp.float32
        )

    def folded_max(x):
        return jnp.max(x.reshape(x.shape[0] // 8, 8, 2 * BLK), axis=0)

    def expo_part(scores, slot, part, largest):
        expo = jnp.exp2((scores - largest) * factor)
        p_ref[slot, edges[part] * BLK : edges[part + 1] * BLK, :] = expo.astype(jnp.bfloat16)

    def value_product(position, slot):
        starts = starts_of(position)
        values = jnp.concatenate([vt_ref[:, pl.ds(start, BLK)] for start in starts], axis=1)
        values = jnp.concatenate([values, jnp.ones((16, NBR * BLK), jnp.bfloat16)], axis=0)
        out = jnp.dot(values, p_ref[slot], preferred_element_type=jnp.float32)
        row_sum = out[2 * HD : 2 * HD + 1, :]
        inverse = 1.0 / row_sum
        for h in range(2):
            part = slice(h * HD, (h + 1) * HD)
            mine = out[part, part] * inverse[:, part]
            rows = pl.ds(pl.multiple_of(position * BLK, BLK), BLK)
            o_ref[rows, part] = mine.T.astype(jnp.bfloat16)
        return row_sum

    def first_part(position, slot):
        scores = score_part(diagonal(position), starts_of(position), 0)
        s_ref[slot, : scores.shape[0], :] = scores
        m_ref[slot] = folded_max(scores)

    def step(position, slot):
        largest = jnp.max(m_ref[slot], axis=0, keepdims=True)
        diag = diagonal(position)
        starts = starts_of(position)
        expo_part(s_ref[slot, : edges[1] * BLK, :], slot, 0, largest)
        first_part(jnp.minimum(position + 1, blocks - 1), 1 - slot)
        for part in range(1, parts):
            expo_part(score_part(diag, starts, part), slot, part, largest)
            if part == 1:
                row_sum = value_product(jnp.maximum(position - 1, 0), 1 - slot)
                l_ref[...] = jnp.maximum(l_ref[...], row_sum)

    @pl.when(pl.program_id(0) == 0)
    def _():
        p_ref[1] = jnp.ones_like(p_ref[1])

    l_ref[...] = jnp.zeros_like(l_ref)
    first_part(0, 0)

    @pl.loop(0, blocks // unroll)
    def _(index):
        for i in range(unroll):
            step(index * unroll + i, i % 2)

    row_sum = value_product(blocks - 1, 1)
    row_sum = jnp.maximum(l_ref[...], row_sum)

    @pl.when(jnp.logical_not(jnp.max(row_sum) < LARGE))
    def _():
        @pl.loop(0, blocks)
        def _(position):
            diag = diagonal(position)
            starts = starts_of(position)
            top = None
            for part in range(parts):
                scores = score_part(diag, starts, part)
                s_ref[part, : scores.shape[0], :] = scores
                some = folded_max(scores)
                top = some if top is None else jnp.maximum(top, some)
            largest = jnp.max(top, axis=0, keepdims=True)
            for part in range(parts):
                size = (edges[part + 1] - edges[part]) * BLK
                expo_part(s_ref[part, :size, :], 1, part, largest)
            value_product(position, 1)


def attend(lists, q, k, vt, first, blocks):
    rows = blocks * BLK
    pair = 2 * HD
    keys = NBR * BLK
    return pl.pallas_call(
        functools.partial(attend_kernel, first, blocks),
        grid_spec=pltpu.PrefetchScalarGridSpec(
            num_scalar_prefetch=1,
            grid=(D // pair,),
            in_specs=[
                pl.BlockSpec((q.shape[0], pair), lambda i, lists: (0, i)),
                pl.BlockSpec((3 * PLANE, pair), lambda i, lists: (0, i)),
                pl.BlockSpec((pair, 3 * PLANE), lambda i, lists: (i, 0)),
            ],
            out_specs=pl.BlockSpec((rows, pair), lambda i, lists: (0, i)),
            scratch_shapes=[
                pltpu.VMEM((3, 5 * BLK, pair), jnp.float32),
                pltpu.VMEM((2, keys, pair), jnp.bfloat16),
                pltpu.VMEM((2, 8, pair), jnp.float32),
                pltpu.VMEM((1, pair), jnp.float32),
            ],
        ),
        out_shape=jax.ShapeDtypeStruct((rows, D), jnp.bfloat16),
        compiler_params=pltpu.CompilerParams(vmem_limit_bytes=VMEM_LIMIT),
        cost_estimate=pl.CostEstimate(
            flops=4 * rows * keys * D, bytes_accessed=32 * MIB, transcendentals=rows * keys * HEADS
        ),
        name="attend",
    )(lists, q, k, vt)


def local(tokens, w_qkv, w_out, neighbours):
    head_count = lax.axis_size("head")
    seq_count = lax.axis_size("seq")
    rows = tokens.shape[0]
    blocks = rows // BLK
    seq = lax.axis_index("seq")
    head = lax.axis_index("head")
    per_plane = PLANE // rows
    side = head // per_plane
    plane = 2 * seq + side
    tie = lax.optimization_barrier

    hops = []
    for s in range(seq_count):
        for h in range(head_count):
            step = 1 if h < per_plane else -1
            hops.append((s * head_count + h, (s + step) % seq_count * head_count + h))

    def forward(x):
        return lax.ppermute(x, ("seq", "head"), hops)

    planes = 2 * seq_count
    lists = lax.dynamic_slice_in_dim(neighbours, head * blocks, blocks, axis=0)
    offset = jnp.mod(lists // PB - plane + 1, planes) - 1
    toward = jnp.where(side == 0, 1, -1)
    slot = jnp.where(offset == 0, 0, jnp.where(offset == toward, 1, 2))
    lists = slot * PB + lists % PB

    w = lax.all_gather(w_qkv, "seq", axis=0, tiled=True)

    if head_count != 2:
        slab = lax.all_gather(tokens, "head", axis=0, tiled=True)
        own = lax.dynamic_slice_in_dim(slab, side * PLANE, PLANE, axis=0)
        other = lax.dynamic_slice_in_dim(slab, (1 - side) * PLANE, PLANE, axis=0)
        far = forward(other)
        q, k, vt = project_own(own, other, w)
        k, w_last = tie((k, w_out))
        k, vt = project_halo([([far], 2 * PLANE)], w, k, vt)
        q = lax.dynamic_slice_in_dim(q, head % per_plane * rows, rows, axis=0)
    else:
        cuts = [0]
        for size in CUTS:
            cuts.append(cuts[-1] + size)

        def swap(x):
            return lax.ppermute(x, "head", [(0, 1), (1, 0)])

        first = tokens[: cuts[1]]
        rest, first = tie((tokens, first))
        x_0 = swap(first)
        later = [rest[start:stop] for start, stop in zip(cuts[1:], cuts[2:])]
        x_0, *later = tie((x_0, *later))
        x_1, x_2 = [swap(part) for part in later]
        far_0 = forward(x_0)
        q, k, vt = project_own(tokens, x_0, w)
        x_1, x_2, k, vt, w_last = tie((x_1, x_2, k, vt, w_out))
        far_1, far_2 = forward(x_1), forward(x_2)
        k, vt = project_halo([([far_0], 2 * PLANE), ([x_1, x_2], PLANE + cuts[1])], w, k, vt)
        k, vt = project_halo([([far_1, far_2], 2 * PLANE + cuts[1])], w, k, vt)
    w_last = lax.all_gather(w_last, "seq", axis=0, tiled=True)
    attended = attend(lists, q, k, vt, 0, blocks)
    return project_update(attended, w_last)


def solution(mesh):
    return jax.shard_map(
        local,
        mesh=mesh,
        in_specs=(P(("seq", "head"), None), P("seq", None), P("seq", None), P("seq", None)),
        out_specs=P(("seq", "head"), None),
        check_vma=False,
    )
```

```python
import functools
import math

import jax
import jax.numpy as jnp
from jax import lax
from jax.experimental import pallas as pl
from jax.experimental.pallas import tpu as pltpu
from jax.sharding import PartitionSpec as P

HEADS = 8
HD = 128
BLK = 128
NBR = 12
PB = 16
D = HEADS * HD
PLANE = PB * BLK
TILE = 512
CUTS = (1280, 512, 256)
STEP = 512
LARGE = 2.0**100
MIB = 1 << 20
VMEM_LIMIT = 54 * MIB


def project_own_kernel(x_ref, w_ref, q_ref, k_ref, vt_ref):
    x = x_ref[...]

    def part(start):
        product = jnp.dot(x, w_ref[:, start : start + 512], preferred_element_type=jnp.float32)
        return product.astype(jnp.bfloat16)

    for col in range(0, D, 512):
        q_ref[:, col : col + 512] = part(col)
        k_ref[:, col : col + 512] = part(D + col)
        vt_ref[col : col + 512, :] = part(2 * D + col).T


def project_cost(rows, columns):
    return pl.CostEstimate(
        flops=2 * rows * D * columns, bytes_accessed=2 * rows * (D + columns), transcendentals=0
    )


def project_own(x, w):
    row_spec = pl.BlockSpec((TILE, D), lambda i: (i, 0))
    return pl.pallas_call(
        project_own_kernel,
        grid=(PLANE // TILE,),
        in_specs=[row_spec, pl.BlockSpec(memory_space=pltpu.VMEM)],
        out_specs=[row_spec, row_spec, pl.BlockSpec((D, TILE), lambda i: (0, i))],
        out_shape=[
            jax.ShapeDtypeStruct((PLANE, D), jnp.bfloat16),
            jax.ShapeDtypeStruct((3 * PLANE, D), jnp.bfloat16),
            jax.ShapeDtypeStruct((D, 3 * PLANE), jnp.bfloat16),
        ],
        compiler_params=pltpu.CompilerParams(vmem_limit_bytes=VMEM_LIMIT),
        cost_estimate=project_cost(PLANE, 3 * D),
        name="project_qkv",
    )(x, w)


def project_halo_kernel(counts, bases, *refs):
    total = sum(counts)
    x_refs, (w_ref, _, _, k_hbm, vt_hbm, k_ref, vt_ref, k_sem, vt_sem) = refs[:total], refs[total:]
    copies = []
    at = 0
    offset = 0
    for i, count in enumerate(counts):
        pieces = [ref[...] for ref in x_refs[at : at + count]]
        at += count
        x = pieces[0] if count == 1 else jnp.concatenate(pieces, axis=0)
        size = x.shape[0]
        rows = pl.ds(offset, size)
        there = pl.ds(bases[i], size)
        offset += size
        for col in range(0, D, 512):
            part = jnp.dot(
                x, w_ref[:, D + col : D + col + 512], preferred_element_type=jnp.float32
            )
            k_ref[rows, col : col + 512] = part.astype(jnp.bfloat16)
        copies.append(pltpu.make_async_copy(k_ref.at[rows, :], k_hbm.at[there, :], k_sem.at[i]))
        copies[-1].start()
        for col in range(0, D, 512):
            part = jnp.dot(
                x, w_ref[:, 2 * D + col : 2 * D + col + 512], preferred_element_type=jnp.float32
            )
            vt_ref[col : col + 512, rows] = part.astype(jnp.bfloat16).T
        copies.append(pltpu.make_async_copy(vt_ref.at[:, rows], vt_hbm.at[:, there], vt_sem.at[i]))
        copies[-1].start()
    for copy in copies:
        copy.wait()


def project_halo(groups, w, k, vt):
    counts = tuple(len(parts) for parts, _ in groups)
    bases = tuple(base for _, base in groups)
    xs = [part for parts, _ in groups for part in parts]
    rows = sum(x.shape[0] for x in xs)
    vmem = pl.BlockSpec(memory_space=pltpu.VMEM)
    hbm = pl.BlockSpec(memory_space=pltpu.HBM)
    return pl.pallas_call(
        functools.partial(project_halo_kernel, counts, bases),
        in_specs=[vmem] * (len(xs) + 1) + [hbm, hbm],
        out_specs=[hbm, hbm],
        out_shape=[
            jax.ShapeDtypeStruct(k.shape, jnp.bfloat16),
            jax.ShapeDtypeStruct(vt.shape, jnp.bfloat16),
        ],
        input_output_aliases={len(xs) + 1: 0, len(xs) + 2: 1},
        scratch_shapes=[
            pltpu.VMEM((rows, D), jnp.bfloat16),
            pltpu.VMEM((D, rows), jnp.bfloat16),
            pltpu.SemaphoreType.DMA((len(groups),)),
            pltpu.SemaphoreType.DMA((len(groups),)),
        ],
        compiler_params=pltpu.CompilerParams(vmem_limit_bytes=40 * MIB),
        cost_estimate=project_cost(rows, 2 * D),
        name="project_kv_halo",
    )(*xs, w, k, vt)


def update_kernel(x_ref, w_ref, o_ref):
    x = x_ref[...]
    for col in range(0, D, STEP):
        part = jnp.dot(x, w_ref[:, col : col + STEP], preferred_element_type=jnp.float32)
        o_ref[:, col : col + STEP] = part.astype(jnp.bfloat16)


def project_update(x, w):
    rows = x.shape[0]
    row_spec = pl.BlockSpec((TILE, D), lambda i: (i, 0))
    return pl.pallas_call(
        update_kernel,
        grid=(rows // TILE,),
        in_specs=[row_spec, pl.BlockSpec(memory_space=pltpu.VMEM)],
        out_specs=row_spec,
        out_shape=jax.ShapeDtypeStruct((rows, D), jnp.bfloat16),
        compiler_params=pltpu.CompilerParams(vmem_limit_bytes=VMEM_LIMIT),
        cost_estimate=project_cost(rows, D),
        name="project_update",
    )(x, w)


def attend_kernel(first, blocks, lists_ref, q_ref, k_ref, vt_ref, o_ref, *scratch):
    s_ref, p_ref, m_ref, l_ref = scratch
    factor = math.log2(math.e) / math.sqrt(HD)
    unroll = 4
    edges = (0, 2, 12)
    parts = len(edges) - 1

    def listed(position):
        return lax.rem(first + position, q_ref.shape[0] // BLK)

    def starts_of(position):
        block = listed(position)
        return [pl.multiple_of(lists_ref[block, j] * BLK, BLK) for j in range(NBR)]

    def diagonal(position):
        q = q_ref[pl.ds(pl.multiple_of(listed(position) * BLK, BLK), BLK), :]
        zero = jnp.zeros((BLK, HD), jnp.bfloat16)
        return jnp.concatenate(
            [
                jnp.concatenate([q[:, :HD], zero], axis=1),
                jnp.concatenate([zero, q[:, HD:]], axis=1),
            ],
            axis=0,
        )

    def score_part(diag, starts, part):
        keys = jnp.concatenate(
            [k_ref[pl.ds(start, BLK), :] for start in starts[edges[part] : edges[part + 1]]], axis=0
        )
        return lax.dot_general(
            keys, diag, (((1,), (1,)), ((), ())), preferred_element_type=jnp.float32
        )

    def folded_max(x):
        return jnp.max(x.reshape(x.shape[0] // 8, 8, 2 * BLK), axis=0)

    def expo_part(scores, slot, part, largest):
        expo = jnp.exp2((scores - largest) * factor)
        p_ref[slot, edges[part] * BLK : edges[part + 1] * BLK, :] = expo.astype(jnp.bfloat16)

    def value_product(position, slot):
        starts = starts_of(position)
        values = jnp.concatenate([vt_ref[:, pl.ds(start, BLK)] for start in starts], axis=1)
        values = jnp.concatenate([values, jnp.ones((16, NBR * BLK), jnp.bfloat16)], axis=0)
        out = jnp.dot(values, p_ref[slot], preferred_element_type=jnp.float32)
        row_sum = out[2 * HD : 2 * HD + 1, :]
        inverse = 1.0 / row_sum
        for h in range(2):
            part = slice(h * HD, (h + 1) * HD)
            mine = out[part, part] * inverse[:, part]
            rows = pl.ds(pl.multiple_of(position * BLK, BLK), BLK)
            o_ref[rows, part] = mine.T.astype(jnp.bfloat16)
        return row_sum

    def first_part(position, slot):
        scores = score_part(diagonal(position), starts_of(position), 0)
        s_ref[slot, : scores.shape[0], :] = scores
        m_ref[slot] = folded_max(scores)

    def step(position, slot):
        largest = jnp.max(m_ref[slot], axis=0, keepdims=True)
        diag = diagonal(position)
        starts = starts_of(position)
        expo_part(s_ref[slot, : edges[1] * BLK, :], slot, 0, largest)
        first_part(jnp.minimum(position + 1, blocks - 1), 1 - slot)
        for part in range(1, parts):
            expo_part(score_part(diag, starts, part), slot, part, largest)
            if part == 1:
                row_sum = value_product(jnp.maximum(position - 1, 0), 1 - slot)
                l_ref[...] = jnp.maximum(l_ref[...], row_sum)

    @pl.when(pl.program_id(0) == 0)
    def _():
        p_ref[1] = jnp.ones_like(p_ref[1])

    l_ref[...] = jnp.zeros_like(l_ref)
    first_part(0, 0)

    @pl.loop(0, blocks // unroll)
    def _(index):
        for i in range(unroll):
            step(index * unroll + i, i % 2)

    row_sum = value_product(blocks - 1, 1)
    row_sum = jnp.maximum(l_ref[...], row_sum)

    @pl.when(jnp.logical_not(jnp.max(row_sum) < LARGE))
    def _():
        @pl.loop(0, blocks)
        def _(position):
            diag = diagonal(position)
            starts = starts_of(position)
            top = None
            for part in range(parts):
                scores = score_part(diag, starts, part)
                s_ref[part, : scores.shape[0], :] = scores
                some = folded_max(scores)
                top = some if top is None else jnp.maximum(top, some)
            largest = jnp.max(top, axis=0, keepdims=True)
            for part in range(parts):
                size = (edges[part + 1] - edges[part]) * BLK
                expo_part(s_ref[part, :size, :], 1, part, largest)
            value_product(position, 1)


def attend(lists, q, k, vt, first, blocks):
    rows = blocks * BLK
    pair = 2 * HD
    keys = NBR * BLK
    return pl.pallas_call(
        functools.partial(attend_kernel, first, blocks),
        grid_spec=pltpu.PrefetchScalarGridSpec(
            num_scalar_prefetch=1,
            grid=(D // pair,),
            in_specs=[
                pl.BlockSpec((q.shape[0], pair), lambda i, lists: (0, i)),
                pl.BlockSpec((3 * PLANE, pair), lambda i, lists: (0, i)),
                pl.BlockSpec((pair, 3 * PLANE), lambda i, lists: (i, 0)),
            ],
            out_specs=pl.BlockSpec((rows, pair), lambda i, lists: (0, i)),
            scratch_shapes=[
                pltpu.VMEM((2, 10 * BLK, pair), jnp.float32),
                pltpu.VMEM((2, keys, pair), jnp.bfloat16),
                pltpu.VMEM((2, 8, pair), jnp.float32),
                pltpu.VMEM((1, pair), jnp.float32),
            ],
        ),
        out_shape=jax.ShapeDtypeStruct((rows, D), jnp.bfloat16),
        compiler_params=pltpu.CompilerParams(vmem_limit_bytes=VMEM_LIMIT),
        cost_estimate=pl.CostEstimate(
            flops=4 * rows * keys * D, bytes_accessed=32 * MIB, transcendentals=rows * keys * HEADS
        ),
        name="attend",
    )(lists, q, k, vt)


def local(tokens, w_qkv, w_out, neighbours):
    head_count = lax.axis_size("head")
    seq_count = lax.axis_size("seq")
    rows = tokens.shape[0]
    blocks = rows // BLK
    seq = lax.axis_index("seq")
    head = lax.axis_index("head")
    per_plane = PLANE // rows
    side = head // per_plane
    plane = 2 * seq + side
    tie = lax.optimization_barrier

    hops = []
    for s in range(seq_count):
        for h in range(head_count):
            step = 1 if h < per_plane else -1
            hops.append((s * head_count + h, (s + step) % seq_count * head_count + h))

    def forward(x):
        return lax.ppermute(x, ("seq", "head"), hops)

    planes = 2 * seq_count
    lists = lax.dynamic_slice_in_dim(neighbours, head * blocks, blocks, axis=0)
    offset = jnp.mod(lists // PB - plane + 1, planes) - 1
    toward = jnp.where(side == 0, 1, -1)
    slot = jnp.where(offset == 0, 0, jnp.where(offset == toward, 1, 2))
    lists = slot * PB + lists % PB

    w = lax.all_gather(w_qkv, "seq", axis=0, tiled=True)

    if head_count != 2:
        slab = lax.all_gather(tokens, "head", axis=0, tiled=True)
        own = lax.dynamic_slice_in_dim(slab, side * PLANE, PLANE, axis=0)
        other = lax.dynamic_slice_in_dim(slab, (1 - side) * PLANE, PLANE, axis=0)
        far = forward(other)
        q, k, vt = project_own(own, w)
        k, vt = project_halo([([other], PLANE)], w, k, vt)
        k, vt = project_halo([([far], 2 * PLANE)], w, k, vt)
        q = lax.dynamic_slice_in_dim(q, head % per_plane * rows, rows, axis=0)
    else:
        cuts = [0]
        for size in CUTS:
            cuts.append(cuts[-1] + size)

        def swap(x):
            return lax.ppermute(x, "head", [(0, 1), (1, 0)])

        first = tokens[: cuts[1]]
        rest, first = tie((tokens, first))
        x_0 = swap(first)
        later = [rest[start:stop] for start, stop in zip(cuts[1:], cuts[2:])]
        x_0, *later = tie((x_0, *later))
        x_1, x_2 = [swap(part) for part in later]
        far_0 = forward(x_0)
        q, k, vt = project_own(tokens, w)
        x_1, k, vt = tie((x_1, k, vt))
        far_1 = forward(x_1)
        k, vt = project_halo([([x_0], PLANE)], w, k, vt)
        x_2, k, vt = tie((x_2, k, vt))
        far_2 = forward(x_2)
        k, vt = project_halo([([far_0], 2 * PLANE), ([x_1, x_2], PLANE + cuts[1])], w, k, vt)
        k, vt = project_halo([([far_1, far_2], 2 * PLANE + cuts[1])], w, k, vt)
    k, w_last = tie((k, w_out))
    w_last = lax.all_gather(w_last, "seq", axis=0, tiled=True)
    attended = attend(lists, q, k, vt, 0, blocks)
    return project_update(attended, w_last)


def solution(mesh):
    return jax.shard_map(
        local,
        mesh=mesh,
        in_specs=(P(("seq", "head"), None), P("seq", None), P("seq", None), P("seq", None)),
        out_specs=P(("seq", "head"), None),
        check_vma=False,
    )
```
